32 devices in a mesh: dom: 8 (over z, x), band: 4 (over y, core).
Axes of the slice: x: 2, y: 2, z: 4, core: 2. Of those that a mesh axis runs over, the one named last changes fastest.
Arguments:
- orbitals_now: bfloat16 [128, 512, 512], P('dom', 'band'), may hold values from -6 to 6
- orbitals_prev: bfloat16 [128, 512, 512], P('dom', 'band'), may hold values from -6 to 6
- interp: bfloat16 [8, 512, 512], replicated, may hold values from -0.25 to 0.25
- owner_map: int32 [128], replicated, may hold values from 0 to 7, as said below
- child_oct: int32 [128, 2], replicated, may hold values from 0 to 7, all different within a row
Outputs:
- predicted: bfloat16 [512, 512, 512], P(('dom', 'band'))
The draws below stay inside these ranges and needn't reach their ends.
Inputs may be any that keep to these rules, and one draw needn't show every extreme that they name: `owner_map`: among the 16 cells of one domain at most 4 have the same owner; in every draw one owner receives exactly 4 cells from every domain.
All inputs are finite; a program needn't handle non-finite values.
Results may differ from the reference program's by a relative error of at most 0.0059.
Values may be sent and summed in bfloat16 or wider, within the bound.
A program may use at most 128 MiB of HBM per device.

```python
import math
import jax
import jax.numpy as jnp
from jax import lax

STATES = 512
NODES = 512
OCTANTS = 8
OLD_DEV = 16
CAP = 4
NEWC_DEV = 64
OLD_CELLS = 128
NEW_CELLS = 512
N_DOM = 8


def draw_owner_map(key, part):
    key_busiest = jax.random.fold_in(key, 11)
    key_ordering = jax.random.fold_in(key, 12)
    key_offset = jax.random.fold_in(key, 13)
    busiest = jax.random.randint(key_busiest, (), 0, N_DOM)
    scores = jax.random.randint(key_ordering, (N_DOM, OLD_DEV), 0, 1 << 20) * OLD_DEV + jnp.arange(OLD_DEV, dtype=jnp.int32)[None, :]
    ordering = jnp.argsort(scores, axis=1)
    cell_ranks = jnp.argsort(ordering, axis=1).astype(jnp.int32)
    offset = jax.random.randint(key_offset, (N_DOM, 1), 0, N_DOM - 1)
    others = (cell_ranks - CAP + offset) % (N_DOM - 1)
    others = others + (others >= busiest).astype(jnp.int32)
    owners = jnp.where(cell_ranks < CAP, busiest, others)
    return owners.reshape(-1).astype(jnp.int32)


def block_levels(stream_key, extent, split, low, high):
    loudness = 1.0
    for axis_at, shards_of in split:
        heights = jax.random.uniform(jax.random.fold_in(jax.random.fold_in(stream_key, 6), axis_at), (shards_of,), jnp.float32, low / len(split), high / len(split))
        loudness = loudness * jnp.repeat(jnp.exp(heights), extent[axis_at] // shards_of).reshape((-1,) + (1,) * (len(extent) - 1 - axis_at))
    return loudness


def choose_distinct(rng, rows, number_of, top, lift):
    ranking = jax.random.permutation(jax.random.fold_in(rng, 1), number_of)
    boost = ranking
    for power in range(3):
        boost = boost * boost // number_of
    boost = boost * lift // number_of
    chance = jax.random.randint(jax.random.fold_in(rng, 2), (rows, number_of), 0, 4096) + boost
    holders = jax.random.permutation(jax.random.fold_in(rng, 3), rows)[jnp.arange(number_of) % rows]
    chance = jnp.where(jnp.arange(rows)[:, None] == holders[None, :], 1 << 14, chance)
    priority = chance * number_of + jnp.arange(number_of)
    return lax.top_k(priority.astype(jnp.int32), top)[1].astype(jnp.int32)


def normal_values(stream_key, extent, deviation, reach, pieces=(), kind=jnp.bfloat16):
    loudness = block_levels(stream_key, extent, pieces, -0.22, 0.18) if pieces else 1.0
    values = jax.random.normal(stream_key, extent, jnp.float32) * deviation * loudness
    return jnp.minimum(jnp.maximum(values, -reach), reach).astype(kind)


def setup_inputs(seed: int = 0) -> dict:
    splits = jax.random.split(jax.random.key(seed), 6)
    orbitals_now = normal_values(splits[0], (OLD_CELLS, STATES, NODES), 1.0, 6.0, ((0, 8), (1, 4)))
    orbitals_prev = normal_values(splits[1], (OLD_CELLS, STATES, NODES), 1.0, 6.0, ((0, 8), (1, 4)))
    interp = normal_values(splits[2], (OCTANTS, NODES, NODES), NODES ** -0.5, 0.25)
    owner_map = draw_owner_map(jax.random.fold_in(splits[5], 71), 0)
    child_oct = choose_distinct(splits[4], OLD_CELLS, OCTANTS, 2, 0)
    return dict(orbitals_now=orbitals_now, orbitals_prev=orbitals_prev, interp=interp, owner_map=owner_map, child_oct=child_oct)


def ranks_of(owners):
    matching = owners[:, :, None] == owners[:, None, :]
    positions = jnp.arange(OLD_DEV, dtype=jnp.int32)
    earlier = positions[None, :] < positions[:, None]
    return lax.optimization_barrier(jnp.sum((matching & earlier[None]).astype(jnp.int32), axis=2)).astype(jnp.int32)

def refine(stacked, octants, interp):

    def refine_cell(inputs):
        parent, picked = inputs
        matrices = interp[picked].astype(jnp.float32)
        return jnp.einsum('sn,jmn->jsm', parent.astype(jnp.float32), matrices).astype(jnp.bfloat16)
    return lax.map(refine_cell, (stacked, octants))

def reference(orbitals_now, orbitals_prev, interp, owner_map, child_oct):
    owners = owner_map.reshape(N_DOM, OLD_DEV).astype(jnp.int32)
    cell_ranks = ranks_of(owners)
    sources = jnp.arange(N_DOM, dtype=jnp.int32)[:, None]
    parent_slot = (owners * NEWC_DEV + (sources * CAP + cell_ranks) * 2).astype(jnp.int32)
    new_index = (parent_slot.reshape(-1, 1) + jnp.arange(2, dtype=jnp.int32)[None, :]).reshape(-1).astype(jnp.int32)
    stacked = jnp.concatenate([orbitals_now, orbitals_prev], axis=1)
    children = refine(stacked, child_oct.astype(jnp.int32), interp)
    cells = children.reshape(-1, 2 * STATES, NODES)

    def accumulate(total, cell):
        return (total + jnp.dot(cell[:STATES], cell[STATES:].T, preferred_element_type=jnp.float32), None)
    zeros_st = jnp.zeros((STATES, STATES), jnp.float32)
    total, _ = lax.scan(accumulate, zeros_st, cells)
    scaling = 1.0 / math.sqrt(2.0 * STATES * OLD_CELLS * NODES)
    intersection_b = (total * scaling).astype(jnp.bfloat16)

    def predict_cell(cell):
        mixed = jnp.dot(intersection_b.T, cell[:STATES], preferred_element_type=jnp.float32)
        return (cell[STATES:].astype(jnp.float32) + mixed).astype(jnp.bfloat16)
    values = lax.map(predict_cell, cells)
    return jnp.zeros((NEW_CELLS, STATES, NODES), jnp.bfloat16).at[new_index].set(values)
```

```python
import functools
import math

import jax
import jax.numpy as jnp
from jax import lax
from jax.experimental import pallas as pl
from jax.experimental.pallas import tpu as pltpu
from jax.sharding import PartitionSpec as P

NT = (((1,), (1,)), ((), ()))
TN = (((0,), (0,)), ((), ()))


def mm(a, b, dims=(((1,), (0,)), ((), ()))):
    return lax.dot_general(a, b, dims, preferred_element_type=jnp.float32)


def gather_band(block):
    band_size = lax.axis_size("band")
    have = {0: block}
    bit = band_size // 2
    while bit:
        perm = [(b, b ^ bit) for b in range(band_size)]
        for off in list(have):
            have[off ^ bit] = lax.ppermute(have[off], "band", perm)
        bit //= 2
    return [have[off] for off in range(band_size)]


def fold_kernel(oct_ref, prev_ref, first_ref, second_ref, out_ref):
    prev = prev_ref[0]
    total = None
    for interp_ref in (first_ref, second_ref):
        child = mm(prev, interp_ref[0], NT).astype(jnp.bfloat16)
        back = mm(child, interp_ref[0])
        total = back if total is None else total + back
    out_ref[0] = total.astype(jnp.bfloat16)


def fold(prev, interp, octants):
    cells, width, nodes = prev.shape
    return pl.pallas_call(
        fold_kernel,
        out_shape=jax.ShapeDtypeStruct(prev.shape, jnp.bfloat16),
        grid_spec=pltpu.PrefetchScalarGridSpec(
            num_scalar_prefetch=1,
            grid=(cells,),
            in_specs=[
                pl.BlockSpec((1, width, nodes), lambda g, o: (g, 0, 0)),
                pl.BlockSpec((1, nodes, nodes), lambda g, o: (o[2 * g], 0, 0)),
                pl.BlockSpec((1, nodes, nodes), lambda g, o: (o[2 * g + 1], 0, 0)),
            ],
            out_specs=pl.BlockSpec((1, width, nodes), lambda g, o: (g, 0, 0)),
        ),
        compiler_params=pltpu.CompilerParams(vmem_limit_bytes=32 * 2**20),
        cost_estimate=pl.CostEstimate(
            flops=8 * cells * width * nodes * nodes,
            bytes_accessed=4 * cells * nodes * (width + nodes),
            transcendentals=0,
        ),
        name="fold",
    )(octants.reshape(-1), prev, interp, interp)


def overlap_kernel(count, *refs):
    now_refs, folded_ref, out_ref = refs[:count], refs[count], refs[count + 1]

    @pl.when(pl.program_id(0) == 0)
    def _():
        out_ref[...] = jnp.zeros_like(out_ref)

    for k in range(count):
        out_ref[k] += mm(now_refs[k][0], folded_ref[0], NT)


def overlap(nows, folded):
    cells, width, nodes = folded.shape
    count = len(nows)
    block = pl.BlockSpec((1, width, nodes), lambda g: (g, 0, 0))
    return pl.pallas_call(
        functools.partial(overlap_kernel, count),
        out_shape=jax.ShapeDtypeStruct((count, width, width), jnp.float32),
        grid=(cells,),
        in_specs=[block] * (count + 1),
        out_specs=pl.BlockSpec((count, width, width), lambda g: (0, 0, 0)),
        compiler_params=pltpu.CompilerParams(vmem_limit_bytes=32 * 2**20),
        name="overlap",
    )(*nows, folded)


def correct_kernel(count, slot_ref, *refs):
    now_refs, prev_ref, mix_ref, out_ref = refs[:count], refs[count], refs[count + 1], refs[count + 2]
    total = prev_ref[0].astype(jnp.float32)
    for k in range(count):
        total = total + mm(mix_ref[k], now_refs[k][0], TN)
    out_ref[0] = total.astype(jnp.bfloat16)


def correct(nows, prev, mix, slot_index, slots):
    cells, width, nodes = prev.shape
    count = len(nows)
    block = pl.BlockSpec((1, width, nodes), lambda g, s: (g, 0, 0))
    return pl.pallas_call(
        functools.partial(correct_kernel, count),
        out_shape=jax.ShapeDtypeStruct((slots, width, nodes), jnp.bfloat16),
        grid_spec=pltpu.PrefetchScalarGridSpec(
            num_scalar_prefetch=1,
            grid=(cells,),
            in_specs=[block] * (count + 1)
            + [pl.BlockSpec((count, width, width), lambda g, s: (0, 0, 0))],
            out_specs=pl.BlockSpec((1, width, nodes), lambda g, s: (s[g], 0, 0)),
        ),
        compiler_params=pltpu.CompilerParams(vmem_limit_bytes=32 * 2**20),
        name="correct",
    )(slot_index, *nows, prev, mix)


def expand_kernel(valid_ref, oct_ref, rows_ref, interp_ref, out_ref):
    band, _, width, nodes = rows_ref.shape
    valid = valid_ref[pl.program_id(0)] > 0

    @pl.when(valid)
    def _():
        for b in range(band):
            out_ref[0, b * width : (b + 1) * width] = mm(
                rows_ref[b, 0], interp_ref[0], NT
            ).astype(jnp.bfloat16)

    @pl.when(jnp.logical_not(valid))
    def _():
        out_ref[...] = jnp.zeros_like(out_ref)


def expand(rows, interp, valid, octants):
    band, slots, width, nodes = rows.shape
    return pl.pallas_call(
        expand_kernel,
        out_shape=jax.ShapeDtypeStruct((2 * slots, band * width, nodes), jnp.bfloat16),
        grid_spec=pltpu.PrefetchScalarGridSpec(
            num_scalar_prefetch=2,
            grid=(slots, 2),
            in_specs=[
                pl.BlockSpec((band, 1, width, nodes), lambda s, j, v, o: (0, s, 0, 0)),
                pl.BlockSpec((1, nodes, nodes), lambda s, j, v, o: (o[2 * s + j], 0, 0)),
            ],
            out_specs=pl.BlockSpec((1, band * width, nodes), lambda s, j, v, o: (2 * s + j, 0, 0)),
        ),
        compiler_params=pltpu.CompilerParams(vmem_limit_bytes=32 * 2**20),
        name="expand",
    )(valid, octants.reshape(-1), rows, interp)


def per_device(orbitals_now, orbitals_prev, interp, owner_map, child_oct):
    dom_size = lax.axis_size("dom")
    band_size = lax.axis_size("band")
    my_dom = lax.axis_index("dom")
    my_band = lax.axis_index("band")
    old_dev, state_dev, node_count = orbitals_now.shape
    states = state_dev * band_size
    capacity = 2 * old_dev // dom_size
    owners = owner_map.reshape(dom_size, old_dev)
    octants = child_oct.reshape(dom_size, old_dev, 2)
    matching = owners[:, :, None] == owners[:, None, :]
    earlier = lax.broadcasted_iota(jnp.int32, (old_dev, old_dev), 1) < lax.broadcasted_iota(
        jnp.int32, (old_dev, old_dev), 0
    )
    ranks = jnp.sum((matching & earlier[None]).astype(jnp.int32), axis=2)
    slot_all = owners * capacity + ranks
    slot_index = lax.dynamic_index_in_dim(slot_all, my_dom, 0, keepdims=False)
    my_octants = lax.dynamic_index_in_dim(octants, my_dom, 0, keepdims=False)
    slot_count = dom_size * capacity // band_size
    source_count = slot_count // capacity
    near = lax.dynamic_slice_in_dim(slot_all, my_band * source_count, source_count, 0)
    near_oct = lax.dynamic_slice_in_dim(octants, my_band * source_count, source_count, 0)
    wanted = my_dom * capacity + jnp.arange(capacity, dtype=jnp.int32)
    hit = (near[:, None, :] == wanted[None, :, None]).astype(jnp.int32)
    valid = jnp.sum(hit, axis=2).reshape(-1)
    slot_oct = jnp.sum(hit[..., None] * near_oct[:, None], axis=2).reshape(-1, 2)

    nows = gather_band(orbitals_now)
    folded = fold(orbitals_prev, interp, my_octants)
    partial = overlap(nows, folded)
    scaling = 1.0 / math.sqrt(2.0 * states * owner_map.shape[0] * node_count)
    mix = (lax.psum(partial, "dom") * scaling).astype(jnp.bfloat16)
    outgoing = correct(nows, orbitals_prev, mix, slot_index, dom_size * capacity)
    received = lax.all_to_all(outgoing, "dom", split_axis=0, concat_axis=0, tiled=True)
    rows = lax.all_to_all(received, "band", split_axis=0, concat_axis=0, tiled=True)
    rows = rows.reshape(band_size, slot_count, state_dev, node_count)
    return expand(rows, interp, valid, slot_oct)


def solution(mesh):
    in_specs = (P("dom", "band", None), P("dom", "band", None), P(), P(), P())
    out_specs = P(("dom", "band"), None, None)
    return jax.shard_map(
        per_device, mesh=mesh, in_specs=in_specs, out_specs=out_specs, check_vma=False
    )
```

```python
import functools
import math

import jax
import jax.numpy as jnp
from jax import lax
from jax.experimental import pallas as pl
from jax.experimental.pallas import tpu as pltpu
from jax.sharding import PartitionSpec as P

NT = (((1,), (1,)), ((), ()))


def mm(a, b, dims=(((1,), (0,)), ((), ()))):
    return lax.dot_general(a, b, dims, preferred_element_type=jnp.float32)


def gather_band(block, beside):
    band_size = lax.axis_size("band")
    have = {0: block}
    bit = band_size // 2
    while bit:
        perm = [(b, b ^ bit) for b in range(band_size)]
        for off in list(have):
            have[off ^ bit] = lax.ppermute(have[off], "band", perm)
        if 2 * bit == band_size:
            have[bit], beside = lax.optimization_barrier((have[bit], beside))
        bit //= 2
    return [have[off] for off in range(band_size)], beside


def fold_kernel(oct_ref, prev_ref, first_ref, second_ref, out_ref):
    prev = prev_ref[0]
    total = None
    for interp_ref in (first_ref, second_ref):
        child = mm(prev, interp_ref[0], NT).astype(jnp.bfloat16)
        back = mm(child, interp_ref[0])
        total = back if total is None else total + back
    out_ref[0] = total.astype(jnp.bfloat16)


def fold(prev, interp, octants):
    cells, width, nodes = prev.shape
    return pl.pallas_call(
        fold_kernel,
        out_shape=jax.ShapeDtypeStruct(prev.shape, jnp.bfloat16),
        grid_spec=pltpu.PrefetchScalarGridSpec(
            num_scalar_prefetch=1,
            grid=(cells,),
            in_specs=[
                pl.BlockSpec((1, width, nodes), lambda g, o: (g, 0, 0)),
                pl.BlockSpec((1, nodes, nodes), lambda g, o: (o[2 * g], 0, 0)),
                pl.BlockSpec((1, nodes, nodes), lambda g, o: (o[2 * g + 1], 0, 0)),
            ],
            out_specs=pl.BlockSpec((1, width, nodes), lambda g, o: (g, 0, 0)),
        ),
        compiler_params=pltpu.CompilerParams(vmem_limit_bytes=32 * 2**20),
        cost_estimate=pl.CostEstimate(
            flops=8 * cells * width * nodes * nodes,
            bytes_accessed=4 * cells * nodes * (width + nodes),
            transcendentals=0,
        ),
        name="fold",
    )(octants.reshape(-1), prev, interp, interp)


def overlap_kernel(count, *refs):
    now_refs, folded_ref, out_ref = refs[:count], refs[count], refs[count + 1]

    @pl.when(pl.program_id(0) == 0)
    def _():
        out_ref[...] = jnp.zeros_like(out_ref)

    for k in range(count):
        total = out_ref[k]
        for at in range(folded_ref.shape[0]):
            total = total + mm(now_refs[k][at], folded_ref[at], NT)
        out_ref[k] = total


def overlap(nows, folded):
    cells, width, nodes = folded.shape
    count = len(nows)
    group = math.gcd(cells, 4)
    block = pl.BlockSpec((group, width, nodes), lambda g: (g, 0, 0))
    return pl.pallas_call(
        functools.partial(overlap_kernel, count),
        out_shape=jax.ShapeDtypeStruct((count, width, width), jnp.float32),
        grid=(cells // group,),
        in_specs=[block] * (count + 1),
        out_specs=pl.BlockSpec((count, width, width), lambda g: (0, 0, 0)),
        compiler_params=pltpu.CompilerParams(vmem_limit_bytes=32 * 2**20),
        name="overlap",
    )(*nows, folded)


def flip(index, mask, size):
    bit = 1
    while bit < size:
        if mask & bit:
            index = index + bit * (1 - 2 * ((index // bit) % 2))
        bit *= 2
    return index


def peer(dom, band):
    return {"dom": dom, "band": band}


def total_kernel(size, scale, part_ref, out_ref, inbox, piece, send_a, recv_a, send_b, recv_b):
    me = lax.axis_index("dom")
    band = lax.axis_index("band")
    rows = part_ref.shape[0] // size
    barrier = pltpu.get_barrier_semaphore()
    for k in range(1, size):
        pl.semaphore_signal(
            barrier, inc=1, device_id=peer(flip(me, k, size), band), device_id_type=pl.DeviceIdType.MESH
        )
    pl.semaphore_wait(barrier, size - 1)

    def chunk(at):
        return pl.ds(pl.multiple_of(at * rows, rows), rows)

    order = list(range(size - 1, 0, -1))
    scatter = {}
    for k in order:
        other = flip(me, k, size)
        scatter[k] = pltpu.make_async_remote_copy(
            src_ref=part_ref.at[chunk(other)],
            dst_ref=inbox.at[k],
            send_sem=send_a.at[k],
            recv_sem=recv_a.at[k],
            device_id=peer(other, band),
            device_id_type=pl.DeviceIdType.MESH,
        )
        scatter[k].start()
    total = part_ref[chunk(me)]
    for k in reversed(order):
        scatter[k].wait_recv()
        total = total + inbox[k]
    piece[...] = (total * scale).astype(jnp.bfloat16)
    spread = {}
    for k in order:
        spread[k] = pltpu.make_async_remote_copy(
            src_ref=piece,
            dst_ref=out_ref.at[chunk(me)],
            send_sem=send_b.at[k],
            recv_sem=recv_b.at[k],
            device_id=peer(flip(me, k, size), band),
            device_id_type=pl.DeviceIdType.MESH,
        )
        spread[k].start()
    out_ref[chunk(me)] = piece[...]
    for k in order:
        scatter[k].wait_send()
        spread[k].wait()


def total_over_dom(part, scale):
    size = lax.axis_size("dom")
    rows, width = part.shape
    return pl.pallas_call(
        functools.partial(total_kernel, size, scale),
        out_shape=jax.ShapeDtypeStruct(part.shape, jnp.bfloat16),
        in_specs=[pl.BlockSpec(memory_space=pltpu.VMEM)],
        out_specs=pl.BlockSpec(memory_space=pltpu.VMEM),
        scratch_shapes=[
            pltpu.VMEM((size, rows // size, width), jnp.float32),
            pltpu.VMEM((rows // size, width), jnp.bfloat16),
        ]
        + [pltpu.SemaphoreType.DMA((size,))] * 4,
        compiler_params=pltpu.CompilerParams(
            collective_id=0, has_side_effects=True, vmem_limit_bytes=32 * 2**20
        ),
        name="total",
    )(part)


def exchange_kernel(size, bands, window, src_ref, out_ref, mid, send_a, recv_a, send_b, recv_b, local):
    me = lax.axis_index("dom")
    band = lax.axis_index("band")
    cap = src_ref.shape[0] // size
    sources = size // bands
    barrier = pltpu.get_barrier_semaphore()
    for k in range(1, size):
        pl.semaphore_signal(
            barrier, inc=1, device_id=peer(flip(me, k, size), band), device_id_type=pl.DeviceIdType.MESH
        )
    for k in range(1, bands):
        pl.semaphore_signal(
            barrier, inc=1, device_id=peer(me, flip(band, k, bands)), device_id_type=pl.DeviceIdType.MESH
        )
    pl.semaphore_wait(barrier, size + bands - 2)

    def over_dom(k):
        other = flip(me, k, size)
        return pltpu.make_async_remote_copy(
            src_ref=src_ref.at[pl.ds(other * cap, cap)],
            dst_ref=mid.at[k],
            send_sem=send_a.at[k],
            recv_sem=recv_a.at[k],
            device_id=peer(other, band),
            device_id_type=pl.DeviceIdType.MESH,
        )

    def place(k):
        source = flip(me, k, size)
        block = mid.at[k] if k else src_ref.at[pl.ds(me * cap, cap)]
        return block, source // sources, source % sources

    def stay(k):
        block, _, at = place(k)
        return pltpu.make_async_copy(block, out_ref.at[band, pl.ds(at * cap, cap)], local.at[k])

    def over_band(k):
        block, target, at = place(k)
        return pltpu.make_async_remote_copy(
            src_ref=block,
            dst_ref=out_ref.at[band, pl.ds(at * cap, cap)],
            send_sem=send_b.at[k],
            recv_sem=recv_b.at[band, at],
            device_id=peer(me, target),
            device_id_type=pl.DeviceIdType.MESH,
        )

    def pass_on(k):
        _, target, _ = place(k)

        @pl.when(target == band)
        def _():
            stay(k).start()

        @pl.when(target != band)
        def _():
            over_band(k).start()

    far = list(range(size // 2, size))
    near = list(range(size // 2 - 1, 0, -1))
    order = []
    for at in range(len(far)):
        order.append(far[at])
        if at < len(near):
            order.append(near[at])
    for k in order[:window]:
        over_dom(k).start()
    pass_on(0)
    for at, k in enumerate(order):
        over_dom(k).wait_recv()
        pass_on(k)
        over_dom(k).wait_send()
        if at + window < len(order):
            over_dom(order[at + window]).start()
    for k in range(size):
        _, target, _ = place(k)

        @pl.when(target == band)
        def _():
            stay(k).wait()

        @pl.when(target != band)
        def _():
            over_band(k).wait_send()

    for k in range(1, bands):
        giver = flip(band, k, bands)
        for at in range(sources):
            pltpu.make_async_remote_copy(
                src_ref=src_ref.at[pl.ds(at * cap, cap)],
                dst_ref=out_ref.at[giver, pl.ds(at * cap, cap)],
                send_sem=send_b.at[0],
                recv_sem=recv_b.at[giver, at],
                device_id=peer(me, giver),
                device_id_type=pl.DeviceIdType.MESH,
            ).wait_recv()


def exchange(outgoing):
    size, bands = lax.axis_size("dom"), lax.axis_size("band")
    slots, width, nodes = outgoing.shape
    cap, sources = slots // size, size // bands
    return pl.pallas_call(
        functools.partial(exchange_kernel, size, bands, 3),
        out_shape=jax.ShapeDtypeStruct((bands, slots // bands, width, nodes), outgoing.dtype),
        in_specs=[pl.BlockSpec(memory_space=pl.ANY)],
        out_specs=pl.BlockSpec(memory_space=pl.ANY),
        scratch_shapes=[pltpu.VMEM((size, cap, width, nodes), outgoing.dtype)]
        + [pltpu.SemaphoreType.DMA((size,))] * 3
        + [pltpu.SemaphoreType.DMA((bands, sources)), pltpu.SemaphoreType.DMA((size,))],
        compiler_params=pltpu.CompilerParams(
            collective_id=1, has_side_effects=True, vmem_limit_bytes=32 * 2**20
        ),
        name="exchange",
    )(outgoing)


def correct_kernel(count, slot_ref, *refs):
    now_refs, prev_ref, mix_ref, out_ref = refs[:count], refs[count], refs[count + 1], refs[count + 2]
    total = prev_ref[0].astype(jnp.float32)
    for k in range(count):
        total = total + mm(mix_ref[k], now_refs[k][0])
    out_ref[0] = total.astype(jnp.bfloat16)


def correct(nows, prev, mix, slot_index, slots):
    cells, width, nodes = prev.shape
    count = len(nows)
    block = pl.BlockSpec((1, width, nodes), lambda g, s: (g, 0, 0))
    return pl.pallas_call(
        functools.partial(correct_kernel, count),
        out_shape=jax.ShapeDtypeStruct((slots, width, nodes), jnp.bfloat16),
        grid_spec=pltpu.PrefetchScalarGridSpec(
            num_scalar_prefetch=1,
            grid=(cells,),
            in_specs=[block] * (count + 1)
            + [pl.BlockSpec((count, width, width), lambda g, s: (0, 0, 0))],
            out_specs=pl.BlockSpec((1, width, nodes), lambda g, s: (s[g], 0, 0)),
        ),
        compiler_params=pltpu.CompilerParams(vmem_limit_bytes=32 * 2**20),
        name="correct",
    )(slot_index, *nows, prev, mix)


def expand_kernel(valid_ref, oct_ref, rows_ref, interp_ref, out_ref):
    band, _, width, nodes = rows_ref.shape
    valid = valid_ref[pl.program_id(0)] > 0

    @pl.when(valid)
    def _():
        for b in range(band):
            out_ref[0, b * width : (b + 1) * width] = mm(
                rows_ref[b, 0], interp_ref[0], NT
            ).astype(jnp.bfloat16)

    @pl.when(jnp.logical_not(valid))
    def _():
        out_ref[...] = jnp.zeros_like(out_ref)


def expand(rows, interp, valid, octants):
    band, slots, width, nodes = rows.shape
    return pl.pallas_call(
        expand_kernel,
        out_shape=jax.ShapeDtypeStruct((2 * slots, band * width, nodes), jnp.bfloat16),
        grid_spec=pltpu.PrefetchScalarGridSpec(
            num_scalar_prefetch=2,
            grid=(slots, 2),
            in_specs=[
                pl.BlockSpec((band, 1, width, nodes), lambda s, j, v, o: (0, s, 0, 0)),
                pl.BlockSpec((1, nodes, nodes), lambda s, j, v, o: (o[2 * s + j], 0, 0)),
            ],
            out_specs=pl.BlockSpec((1, band * width, nodes), lambda s, j, v, o: (2 * s + j, 0, 0)),
        ),
        compiler_params=pltpu.CompilerParams(vmem_limit_bytes=32 * 2**20),
        name="expand",
    )(valid, octants.reshape(-1), rows, interp)


def per_device(orbitals_now, orbitals_prev, interp, owner_map, child_oct):
    dom_size = lax.axis_size("dom")
    band_size = lax.axis_size("band")
    my_dom = lax.axis_index("dom")
    my_band = lax.axis_index("band")
    old_dev, state_dev, node_count = orbitals_now.shape
    states = state_dev * band_size
    capacity = 2 * old_dev // dom_size
    owners = owner_map.reshape(dom_size, old_dev)
    octants = child_oct.reshape(dom_size, old_dev, 2)
    matching = owners[:, :, None] == owners[:, None, :]
    earlier = lax.broadcasted_iota(jnp.int32, (old_dev, old_dev), 1) < lax.broadcasted_iota(
        jnp.int32, (old_dev, old_dev), 0
    )
    ranks = jnp.sum((matching & earlier[None]).astype(jnp.int32), axis=2)
    slot_all = owners * capacity + ranks
    slot_index = lax.dynamic_index_in_dim(slot_all, my_dom, 0, keepdims=False)
    my_octants = lax.dynamic_index_in_dim(octants, my_dom, 0, keepdims=False)
    slot_count = dom_size * capacity // band_size
    source_count = slot_count // capacity
    near = lax.dynamic_slice_in_dim(slot_all, my_band * source_count, source_count, 0)
    near_oct = lax.dynamic_slice_in_dim(octants, my_band * source_count, source_count, 0)
    wanted = my_dom * capacity + jnp.arange(capacity, dtype=jnp.int32)
    hit = (near[:, None, :] == wanted[None, :, None]).astype(jnp.int32)
    valid = jnp.sum(hit, axis=2).reshape(-1)
    slot_oct = jnp.sum(hit[..., None] * near_oct[:, None], axis=2).reshape(-1, 2)

    folded = fold(orbitals_prev, interp, my_octants)
    nows, folded = gather_band(orbitals_now, folded)
    partial = overlap(nows, folded)
    scaling = 1.0 / math.sqrt(2.0 * states * owner_map.shape[0] * node_count)
    mix = total_over_dom(partial.reshape(states, state_dev), scaling)
    mix = jnp.swapaxes(mix.reshape(partial.shape), 1, 2)
    outgoing = correct(nows, orbitals_prev, mix, slot_index, dom_size * capacity)
    rows = exchange(outgoing)
    return expand(rows, interp, valid, slot_oct)


def solution(mesh):
    in_specs = (P("dom", "band", None), P("dom", "band", None), P(), P(), P())
    out_specs = P(("dom", "band"), None, None)
    return jax.shard_map(
        per_device, mesh=mesh, in_specs=in_specs, out_specs=out_specs, check_vma=False
    )
```
